32 devices in a mesh: row: 8 (over z, core), pair: 4 (over y, x).
Axes of the slice: x: 2, y: 2, z: 4, core: 2. Of those that a mesh axis runs over, the one named last changes fastest.
Arguments:
- slab: float32 [2048, 2048], P(('row', 'pair'))
- plan: int32 [2, 8], replicated, may hold values from 0 to 7, as said below
Outputs:
- rotated: float32 [2048, 2048], P(('row', 'pair'))
- sing_vals: float32 [2048], replicated
The draws below stay inside these ranges and needn't reach their ends.
Inputs may be any that keep to these rules, and one draw needn't show every extreme that they name: Each row of plan is a permutation of the block ids; no two blocks form a pair in two rounds, and the two blocks of a pair in round r sit in two different pairs in round r + 1.
All inputs are finite; a program needn't handle non-finite values.
Results may differ from the reference program's by a relative error of at most 0.00017.
Values sent between devices are 32-bit elements; how exact they have to be, the bound alone decides.
No kernel may reach another device: no remote copies, remote signals or barrier semaphores. Data moves between devices by JAX's collectives and lax.ppermute only.
A program may use at most 64 MiB of HBM per device.

```python
import math
import jax
import jax.numpy as jnp
from jax import lax

BLK = 256
ROUNDS = 2
NS_STEPS = 4
NCOL = 2048
ROWS = 2048


def draw_slab(key, part):
    k_noise, k_common, k_cols = jax.random.split(jax.random.fold_in(key, 11), 3)
    noise = jax.random.normal(k_noise, (ROWS, NCOL), jnp.float32)
    common = jax.random.normal(k_common, (ROWS, BLK), jnp.float32)
    mixing = 0.5
    col_scale = jnp.exp(jax.random.uniform(k_cols, (1, NCOL), jnp.float32, math.log(0.5), math.log(2.0)))
    shared = jnp.tile(common, (1, NCOL // BLK))
    return ((noise + mixing * shared) * col_scale).astype(jnp.float32)


def draw_plan(key, part):
    k_labels, k_start, k_order = jax.random.split(jax.random.fold_in(key, 7), 3)
    nblocks = NCOL // BLK
    circle = nblocks - 1
    labels = jax.random.permutation(k_labels, nblocks).astype(jnp.int32)
    start = jax.random.randint(k_start, (), 0, circle, dtype=jnp.int32)
    steps_k = jnp.arange(1, nblocks // 2, dtype=jnp.int32)
    result = []
    for rnd in range(ROUNDS):
        turn_t = (start + rnd) % circle
        first = jnp.concatenate([jnp.full((1,), circle, jnp.int32), (turn_t + steps_k) % circle])
        second = jnp.concatenate([jnp.full((1,), 1, jnp.int32) * turn_t, (turn_t - steps_k + circle) % circle])
        order = jax.random.permutation(jax.random.fold_in(k_order, rnd), nblocks // 2)
        slots = jnp.stack([first[order], second[order]], axis=1).reshape(nblocks)
        result.append(labels[slots])
    return jnp.stack(result).astype(jnp.int32)


def setup_inputs(seed: int = 0) -> dict:
    splits = jax.random.split(jax.random.key(seed), 3)
    slab = draw_slab(jax.random.fold_in(splits[2], 71), 0)
    plan = draw_plan(jax.random.fold_in(splits[2], 71), 0)
    return dict(slab=slab, plan=plan)


HIGH = lax.Precision.HIGHEST

def position(order):
    count = order.shape[0]
    slots = jnp.arange(count, dtype=jnp.int32)
    return lax.optimization_barrier(jnp.sum(jnp.where(order[None, :] == slots[:, None], slots[None, :], 0), axis=1)).astype(jnp.int32)

def rotation(gram, width):
    diag_vals = jnp.diagonal(gram)
    coupling = gram[:width, width:] / (diag_vals[:width, None] + diag_vals[None, width:] + 1e-06)
    zero_part = jnp.zeros((width, width), jnp.float32)
    skew = jnp.concatenate([jnp.concatenate([zero_part, coupling], 1), jnp.concatenate([-coupling.T, zero_part], 1)], 0)
    scale_c = jnp.sqrt(1.0 + jnp.sum(coupling * coupling))
    ident = jnp.eye(2 * width, dtype=jnp.float32)
    turn = (ident + skew) / scale_c
    for step in range(NS_STEPS):
        inner = jnp.dot(turn.T, turn, precision=HIGH, preferred_element_type=jnp.float32)
        turn = 0.5 * jnp.dot(turn, 3.0 * ident - inner, precision=HIGH, preferred_element_type=jnp.float32)
    return turn

def reference(slab, plan):
    total_rows = slab.shape[0]
    nblocks = NCOL // BLK
    blocks = slab.reshape(total_rows, nblocks, BLK)
    current = jnp.take(blocks, plan[0], axis=1)
    for rnd in range(ROUNDS):
        if rnd > 0:
            current = jnp.take(current, position(plan[rnd - 1])[plan[rnd]], axis=1)
        pairs = current.reshape(total_rows, nblocks // 2, 2 * BLK).transpose(1, 0, 2)

        def one_pair(matrix):
            gram = jnp.dot(matrix.T, matrix, precision=HIGH, preferred_element_type=jnp.float32)
            return jnp.dot(matrix, rotation(gram, BLK), precision=HIGH, preferred_element_type=jnp.float32)
        pairs = lax.map(one_pair, pairs)
        current = pairs.transpose(1, 0, 2).reshape(total_rows, nblocks, BLK)
    rotated = jnp.take(current, position(plan[ROUNDS - 1]), axis=1).reshape(total_rows, NCOL)
    sing_vals = jnp.sqrt(lax.optimization_barrier(jnp.sum(rotated * rotated, axis=0)) / total_rows)
    return (rotated, sing_vals)
```

```python
import functools

import jax
import jax.numpy as jnp
from jax import lax
from jax.experimental import pallas as pl
from jax.experimental.pallas import tpu as pltpu
from jax.sharding import PartitionSpec as P

NS_STEPS = 4
PAD = 8

VMEM = pl.BlockSpec(memory_space=pltpu.VMEM)
SMEM = pl.BlockSpec(memory_space=pltpu.SMEM)
ROWS_BY_COLS = (((1,), (0,)), ((), ()))
COLS_BY_COLS = (((0,), (0,)), ((), ()))


def split(x):
    high = x.astype(jnp.bfloat16)
    return high, (x - high.astype(jnp.float32)).astype(jnp.bfloat16)


def mul(a, b, dims=ROWS_BY_COLS):
    dot = functools.partial(lax.dot_general, dimension_numbers=dims, preferred_element_type=jnp.float32)
    return dot(a[0], b[0]) + (dot(a[0], b[1]) + dot(a[1], b[0]))


def where_is(plan_ref, rnd, block, count):
    found = jnp.int32(0)
    for slot in range(count):
        found = jnp.where(plan_ref[rnd, slot] == block, slot // 2, found)
    return found


def deal_kernel(plan_ref, slab_ref, *outs):
    me = lax.axis_index("pair")
    width = outs[0].shape[1] // 2
    for mask, out in enumerate(outs):
        to = me ^ mask
        for half in range(2):
            block = plan_ref[0, 2 * to + half]
            start = pl.multiple_of(block * width, width)
            out[:, half * width : (half + 1) * width] = slab_ref[:, pl.ds(start, width)]


def cross_of(first, second, keep_ref, send_ref, scratch):
    width = first.shape[1]
    scratch[...] = mul(split(first), split(second), COLS_BY_COLS)
    diag = jnp.concatenate(
        [
            jnp.sum(first * first, axis=0, keepdims=True),
            jnp.sum(second * second, axis=0, keepdims=True),
            jnp.zeros((PAD - 2, width), jnp.float32),
        ],
        axis=0,
    )
    core = lax.axis_index("row") & 1
    part = width // 2
    for ref, which in ((keep_ref, core), (send_ref, 1 - core)):
        ref[:part, :] = scratch[pl.ds(pl.multiple_of(which * part, part), part), :]
        ref[part:, :] = diag


def first_cross_kernel(*refs):
    *ins, local_ref, keep_ref, send_ref, scratch = refs
    me = lax.axis_index("pair")
    rows = ins[0].shape[0]
    width = ins[0].shape[1] // 2
    for mask, ref in enumerate(ins):
        local_ref[pl.ds(pl.multiple_of((me ^ mask) * rows, rows), rows), :] = ref[...]
    cross_of(local_ref[:, :width], local_ref[:, width:], keep_ref, send_ref, scratch)


def next_cross_kernel(plan_ref, *refs, rnd):
    *ins, local_ref, keep_ref, send_ref, scratch = refs
    width = ins[0].shape[1]
    count = 2 * len(ins)
    me = lax.axis_index("pair")
    halves = []
    for half in range(2):
        source = where_is(plan_ref, rnd - 1, plan_ref[rnd, 2 * me + half], count)
        block = ins[0][...]
        for mask in range(1, len(ins)):
            block = jnp.where(source == (me ^ mask), ins[mask][...], block)
        local_ref[:, half * width : (half + 1) * width] = block
        halves.append(block)
    cross_of(halves[0], halves[1], keep_ref, send_ref, scratch)


def rotate(mine, other, first, second):
    part, width = mine.shape[0] - PAD, mine.shape[1]
    core = lax.axis_index("row") & 1
    cross = jnp.concatenate(
        [jnp.where(core == 0, mine[:part], other[:part]), jnp.where(core == 0, other[:part], mine[:part])], axis=0
    )
    diag_first = jnp.transpose(jnp.broadcast_to(mine[part : part + 1], (width, width)))
    diag_second = mine[part + 1 : part + 2]
    coupling = cross / (diag_first + diag_second + 1e-06)
    k = split(coupling)
    kt = split(jnp.transpose(coupling))
    inv_sq = 1.0 / (1.0 + jnp.sum(coupling * coupling))
    row_id = lax.broadcasted_iota(jnp.int32, (width, width), 0)
    col_id = lax.broadcasted_iota(jnp.int32, (width, width), 1)
    ident = jnp.where(row_id == col_id, 1.0, 0.0)
    squares = [(ident + mul(k, kt)) * inv_sq, (ident + mul(kt, k)) * inv_sq]
    moved = [first - mul(split(second), kt), second + mul(split(first), k)]
    factors = [None, None]
    for step in range(NS_STEPS):
        for side in range(2):
            near = split(1.5 * ident - 0.5 * squares[side])
            if step == 0:
                factors[side] = 1.5 * ident - 0.5 * squares[side]
            else:
                factors[side] = mul(split(factors[side]), near)
            if step < NS_STEPS - 1:
                squares[side] = mul(split(mul(split(squares[side]), near)), near)
    scale = jnp.sqrt(inv_sq)
    return [mul(split(moved[side]), split(factors[side])) * scale for side in range(2)]


def turn_kernel(plan_ref, mine_ref, other_ref, local_ref, *outs, rnd):
    width = local_ref.shape[1] // 2
    new = rotate(mine_ref[...], other_ref[...], local_ref[:, :width], local_ref[:, width:])
    me = lax.axis_index("pair")
    to = where_is(plan_ref, rnd + 1, plan_ref[rnd, 2 * me], 2 * len(outs))
    for mask, out in enumerate(outs):
        out[...] = jnp.where(to == (me ^ mask), new[0], new[1])


def last_turn_kernel(mine_ref, other_ref, local_ref, *refs):
    *outs, squares_ref, scratch = refs
    width = local_ref.shape[1] // 2
    new = rotate(mine_ref[...], other_ref[...], local_ref[:, :width], local_ref[:, width:])
    scratch[:, :width] = new[0]
    scratch[:, width:] = new[1]
    squares_ref[...] = jnp.concatenate(
        [jnp.sum(part * part, axis=0, keepdims=True) for part in new] + [jnp.zeros((PAD - 2, width), jnp.float32)],
        axis=0,
    )
    me = lax.axis_index("pair")
    rows = outs[0].shape[0]
    for mask, out in enumerate(outs):
        out[...] = scratch[pl.ds(pl.multiple_of((me ^ mask) * rows, rows), rows), :]


def place_kernel(plan_ref, *refs, rnd):
    *ins, out_ref = refs
    width = ins[0].shape[1] // 2
    me = lax.axis_index("pair")
    for mask, ref in enumerate(ins):
        for half in range(2):
            block = plan_ref[rnd, 2 * (me ^ mask) + half]
            start = pl.multiple_of(block * width, width)
            out_ref[:, pl.ds(start, width)] = ref[:, half * width : (half + 1) * width]


def norms_kernel(plan_ref, *refs, rnd, total_rows):
    *ins, out_ref = refs
    width = ins[0].shape[1]
    me = lax.axis_index("pair")
    for mask, ref in enumerate(ins):
        for half in range(2):
            block = plan_ref[rnd, 2 * (me ^ mask) + half]
            start = pl.multiple_of(block * width, width)
            out_ref[:, pl.ds(start, width)] = jnp.sqrt(ref[half : half + 1, :] / total_rows)


def swap(x, axis, mask):
    return lax.ppermute(x, axis, [(i, i ^ mask) for i in range(lax.axis_size(axis))])


def spread(parts):
    return [parts[0]] + [swap(parts[mask], "pair", mask) for mask in range(1, len(parts))]


def tree_sum(parts):
    while len(parts) > 1:
        parts = [a + b for a, b in zip(parts[::2], parts[1::2])]
    return parts[0]


def over_chips(x):
    return tree_sum([x] + [swap(x, "row", mask) for mask in range(2, lax.axis_size("row"), 2)])


def call(kernel, ins, outs, scratch=(), smem=0):
    shapes = [jax.ShapeDtypeStruct(shape, jnp.float32) for shape in outs]
    return pl.pallas_call(
        kernel,
        out_shape=shapes,
        in_specs=[SMEM] * smem + [VMEM] * (len(ins) - smem),
        out_specs=[VMEM] * len(outs),
        scratch_shapes=[pltpu.VMEM(shape, jnp.float32) for shape in scratch],
        compiler_params=pltpu.CompilerParams(vmem_limit_bytes=24 * 2**20),
    )(*ins)


def on_device(slab, plan):
    piece_rows, ncols = slab.shape
    rounds = plan.shape[0]
    pair_count = lax.axis_size("pair")
    width = ncols // (2 * pair_count)
    group_rows = piece_rows * pair_count
    total_rows = group_rows * lax.axis_size("row")
    part = (width // 2 + PAD, width)
    square = (width, width)

    dealt = call(deal_kernel, [plan, slab], [(piece_rows, 2 * width)] * pair_count, smem=1)
    held = spread(dealt)
    for rnd in range(rounds):
        if rnd == 0:
            local, keep, send = call(first_cross_kernel, held, [(group_rows, 2 * width), part, part], [square])
        else:
            local, keep, send = call(
                functools.partial(next_cross_kernel, rnd=rnd),
                [plan] + held,
                [(group_rows, 2 * width), part, part],
                [square],
                smem=1,
            )
        mine = over_chips(keep + swap(send, "row", 1))
        other = swap(mine, "row", 1)
        if rnd < rounds - 1:
            sent = call(
                functools.partial(turn_kernel, rnd=rnd),
                [plan, mine, other, local],
                [(group_rows, width)] * pair_count,
                smem=1,
            )
            held = spread(sent)
    *sent, squares = call(
        last_turn_kernel,
        [mine, other, local],
        [(piece_rows, 2 * width)] * pair_count + [(PAD, width)],
        [(group_rows, 2 * width)],
    )
    back = spread(sent)
    squares = squares + swap(squares, "row", 1)
    squares = spread([over_chips(squares)] * pair_count)
    (rotated,) = call(functools.partial(place_kernel, rnd=rounds - 1), [plan] + back, [(piece_rows, ncols)], smem=1)
    (norms,) = call(
        functools.partial(norms_kernel, rnd=rounds - 1, total_rows=total_rows), [plan] + squares, [(1, ncols)], smem=1
    )
    return rotated, norms.reshape(ncols)


def solution(mesh):
    specs = (P(("row", "pair"), None), P())
    return jax.shard_map(on_device, mesh=mesh, in_specs=specs, out_specs=specs, check_vma=False)
```

```python
import functools
import itertools
import math

import jax
import jax.numpy as jnp
from jax import lax
from jax.experimental import pallas as pl
from jax.experimental.pallas import tpu as pltpu
from jax.sharding import PartitionSpec as P

NS_STEPS = 4
PAD = 8
MOST_MOVES = 16

VMEM = pl.BlockSpec(memory_space=pltpu.VMEM)
SMEM = pl.BlockSpec(memory_space=pltpu.SMEM)
ROWS_BY_COLS = (((1,), (0,)), ((), ()))
COLS_BY_COLS = (((0,), (0,)), ((), ()))


def split(x):
    high = x.astype(jnp.bfloat16)
    return high, (x - high.astype(jnp.float32)).astype(jnp.bfloat16)


def mul(a, b, dims=ROWS_BY_COLS):
    dot = functools.partial(lax.dot_general, dimension_numbers=dims, preferred_element_type=jnp.float32)
    return dot(a[0], b[0]) + (dot(a[0], b[1]) + dot(a[1], b[0]))


def slot_of(plan_ref, rnd, block, count):
    found = jnp.int32(0)
    for slot in range(1, count):
        found = jnp.where(plan_ref[rnd, slot] == block, slot, found)
    return found


def route_kernel(plan_ref, table_ref, case_ref, *, rnd, moves):
    slots = plan_ref.shape[1]
    count = slots // 2
    now, half, seen = jnp.int32(0), jnp.int32(0), jnp.int32(0)
    for _ in range(count):
        seen = seen | (jnp.int32(1) << now)
        leaves = plan_ref[rnd, 2 * now + 1 - half]
        slot = slot_of(plan_ref, rnd + 1, leaves, slots)
        joins = slot_of(plan_ref, rnd, plan_ref[rnd + 1, slot ^ 1], slots)
        table_ref[0, now] = half
        table_ref[1, now] = slot_of(plan_ref, rnd + 1, plan_ref[rnd, 2 * now + half], slots) // 2
        table_ref[2, now] = joins // 2
        now, half = joins // 2, joins % 2
        closed = ((seen >> now) & 1) == 1
        unseen = jnp.int32(0)
        for device in reversed(range(count)):
            unseen = jnp.where(((seen >> device) & 1) == 0, device, unseen)
        now, half = jnp.where(closed, unseen, now), jnp.where(closed, 0, half)
    code = jnp.int32(0)
    for device in range(count):
        code = code * count + table_ref[2, device]
    case = jnp.int32(0)
    for index, move in enumerate(moves):
        case = jnp.where(code == functools.reduce(lambda total, to: total * count + to, move), index, case)
    case_ref[0, 0] = case


def deal_kernel(plan_ref, slab_ref, *outs):
    me = lax.axis_index("pair")
    width = outs[0].shape[1] // 2
    for mask, out in enumerate(outs):
        to = me ^ mask
        for half in range(2):
            block = plan_ref[0, 2 * to + half]
            start = pl.multiple_of(block * width, width)
            out[:, half * width : (half + 1) * width] = slab_ref[:, pl.ds(start, width)]


def cross_of(first, second, keep_ref, send_ref, scratch):
    width = first.shape[1]
    scratch[...] = mul(split(first), split(second), COLS_BY_COLS)
    diag = jnp.concatenate(
        [
            jnp.sum(first * first, axis=0, keepdims=True),
            jnp.sum(second * second, axis=0, keepdims=True),
            jnp.zeros((PAD - 2, width), jnp.float32),
        ],
        axis=0,
    )
    core = lax.axis_index("row") & 1
    part = width // 2
    for ref, which in ((keep_ref, core), (send_ref, 1 - core)):
        ref[:part, :] = scratch[pl.ds(pl.multiple_of(which * part, part), part), :]
        ref[part:, :] = diag


def first_cross_kernel(*refs):
    *ins, local_ref, keep_ref, send_ref, scratch = refs
    me = lax.axis_index("pair")
    rows = ins[0].shape[0]
    width = ins[0].shape[1] // 2
    for mask, ref in enumerate(ins):
        local_ref[pl.ds(pl.multiple_of((me ^ mask) * rows, rows), rows), :] = ref[...]
    cross_of(local_ref[:, :width], local_ref[:, width:], keep_ref, send_ref, scratch)


def next_cross_kernel(plan_ref, table_ref, kept_ref, *refs, rnd):
    *ins, local_ref, keep_ref, send_ref, scratch = refs
    width = kept_ref.shape[1]
    count = plan_ref.shape[1] // 2
    me = lax.axis_index("pair")
    came = ins[0][...]
    for mask in range(2, len(ins) + 1):
        came = jnp.where(table_ref[2, me ^ mask] == me, ins[mask - 1][...], came)
    kept_first = plan_ref[rnd - 1, 2 * me + table_ref[0, me]] == plan_ref[rnd, 2 * table_ref[1, me]]
    first = jnp.where(kept_first, kept_ref[...], came)
    second = jnp.where(kept_first, came, kept_ref[...])
    local_ref[:, :width] = first
    local_ref[:, width:] = second
    cross_of(first, second, keep_ref, send_ref, scratch)


def rotate(mine, other, first, second):
    part, width = mine.shape[0] - PAD, mine.shape[1]
    core = lax.axis_index("row") & 1
    cross = jnp.concatenate(
        [jnp.where(core == 0, mine[:part], other[:part]), jnp.where(core == 0, other[:part], mine[:part])], axis=0
    )
    diag_first = jnp.transpose(jnp.broadcast_to(mine[part : part + 1], (width, width)))
    diag_second = mine[part + 1 : part + 2]
    coupling = cross / (diag_first + diag_second + 1e-06)
    k = split(coupling)
    kt = split(jnp.transpose(coupling))
    inv_sq = 1.0 / (1.0 + jnp.sum(coupling * coupling))
    row_id = lax.broadcasted_iota(jnp.int32, (width, width), 0)
    col_id = lax.broadcasted_iota(jnp.int32, (width, width), 1)
    ident = jnp.where(row_id == col_id, 1.0, 0.0)
    squares = [(ident + mul(k, kt)) * inv_sq, (ident + mul(kt, k)) * inv_sq]
    moved = [first - mul(split(second), kt), second + mul(split(first), k)]
    factors = [None, None]
    for step in range(NS_STEPS):
        for side in range(2):
            near = split(1.5 * ident - 0.5 * squares[side])
            if step == 0:
                factors[side] = 1.5 * ident - 0.5 * squares[side]
            else:
                factors[side] = mul(split(factors[side]), near)
            if step < NS_STEPS - 1:
                squares[side] = mul(split(mul(split(squares[side]), near)), near)
    scale = jnp.sqrt(inv_sq)
    return [mul(split(moved[side]), split(factors[side])) * scale for side in range(2)]


def turn_kernel(table_ref, mine_ref, other_ref, local_ref, kept_ref, leaves_ref):
    width = local_ref.shape[1] // 2
    new = rotate(mine_ref[...], other_ref[...], local_ref[:, :width], local_ref[:, width:])
    keeps_first = table_ref[0, lax.axis_index("pair")] == 0
    kept_ref[...] = jnp.where(keeps_first, new[0], new[1])
    leaves_ref[...] = jnp.where(keeps_first, new[1], new[0])


def last_turn_kernel(plan_ref, table_ref, mine_ref, other_ref, local_ref, *refs, rnd):
    *outs, squares_ref, scratch = refs
    width = local_ref.shape[1] // 2
    new = rotate(mine_ref[...], other_ref[...], local_ref[:, :width], local_ref[:, width:])
    me = lax.axis_index("pair")
    squares_ref[...] = jnp.zeros_like(squares_ref)
    for half in range(2):
        scratch[:, half * width : (half + 1) * width] = new[half]
        block = plan_ref[rnd, 2 * table_ref[1, me] + half]
        squares_ref[pl.ds(block, 1), :] = jnp.sum(new[half] * new[half], axis=0, keepdims=True)
    rows = outs[0].shape[0]
    for mask, out in enumerate(outs):
        out[...] = scratch[pl.ds(pl.multiple_of((me ^ mask) * rows, rows), rows), :]


def place_kernel(plan_ref, table_ref, *refs, rnd):
    *ins, out_ref = refs
    width = ins[0].shape[1] // 2
    me = lax.axis_index("pair")
    for mask, ref in enumerate(ins):
        for half in range(2):
            block = plan_ref[rnd, 2 * table_ref[1, me ^ mask] + half]
            start = pl.multiple_of(block * width, width)
            out_ref[:, pl.ds(start, width)] = ref[:, half * width : (half + 1) * width]


def swap(x, axis, mask):
    return lax.ppermute(x, axis, [(i, i ^ mask) for i in range(lax.axis_size(axis))])


def spread(parts):
    return [parts[0]] + [swap(parts[mask], "pair", mask) for mask in range(1, len(parts))]


def tree_sum(parts):
    while len(parts) > 1:
        parts = [a + b for a, b in zip(parts[::2], parts[1::2])]
    return parts[0]


def over_chips(x):
    return tree_sum([x] + [swap(x, "row", mask) for mask in range(2, lax.axis_size("row"), 2)])


def powers(size):
    return [1 << bit for bit in range(size.bit_length() - 1)]


def hand_on(x, case, moves):
    if moves:
        ways = [lambda x, move=move: lax.ppermute(x, "pair", list(enumerate(move))) for move in moves]
        return [lax.switch(case, ways, x)]
    return [swap(x, "pair", mask) for mask in range(1, lax.axis_size("pair"))]


def call(kernel, ins, outs, scratch=(), smem=0, smem_outs=(), cost=None):
    shapes = [jax.ShapeDtypeStruct(shape, jnp.int32) for shape in smem_outs]
    shapes += [jax.ShapeDtypeStruct(shape, jnp.float32) for shape in outs]
    return pl.pallas_call(
        kernel,
        out_shape=shapes,
        in_specs=[SMEM] * smem + [VMEM] * (len(ins) - smem),
        out_specs=[SMEM] * len(smem_outs) + [VMEM] * len(outs),
        scratch_shapes=[pltpu.VMEM(shape, jnp.float32) for shape in scratch],
        compiler_params=pltpu.CompilerParams(vmem_limit_bytes=24 * 2**20),
        cost_estimate=cost,
    )(*ins)


def on_device(slab, plan):
    piece_rows, ncols = slab.shape
    pair_count = lax.axis_size("pair")
    blocks = 2 * pair_count
    width = ncols // blocks
    group_rows = piece_rows * pair_count
    total_rows = group_rows * lax.axis_size("row")
    part = (width // 2 + PAD, width)
    square = (width, width)
    block = (group_rows, width)
    local_shape = (group_rows, 2 * width)
    piece = (piece_rows, 2 * width)
    moves = []
    if math.factorial(pair_count) <= 3 * MOST_MOVES:
        moves = [m for m in itertools.permutations(range(pair_count)) if all(to != i for i, to in enumerate(m))]

    dealt = call(deal_kernel, [plan, slab], [piece] * pair_count, smem=1)
    held = spread(dealt)
    table, case = call(
        functools.partial(route_kernel, rnd=0, moves=moves), [plan], [], smem=1, smem_outs=[(3, pair_count), (1, 1)]
    )
    local, keep, send = call(first_cross_kernel, held, [local_shape, part, part], [square])
    mine = over_chips(keep + swap(send, "row", 1))
    other = swap(mine, "row", 1)
    kept, leaves = call(turn_kernel, [table, mine, other, local], [block, block], smem=1)
    came = hand_on(leaves, case[0, 0], moves)
    local, keep, send = call(
        functools.partial(next_cross_kernel, rnd=1),
        [plan, table, kept] + came,
        [local_shape, part, part],
        [square],
        smem=2,
    )
    mine = over_chips(keep + swap(send, "row", 1))
    other = swap(mine, "row", 1)
    *sent, squares = call(
        functools.partial(last_turn_kernel, rnd=1),
        [plan, table, mine, other, local],
        [piece] * pair_count + [(blocks, width)],
        [local_shape],
        smem=2,
    )
    back = [sent[0]]
    hops = [("row", mask) for mask in powers(lax.axis_size("row"))] + [("pair", mask) for mask in powers(pair_count)]
    for hop, (axis, mask) in enumerate(hops[:-1]):
        if hop + 1 < pair_count:
            squares, piece_out = lax.optimization_barrier((squares, sent[hop + 1]))
            back.append(swap(piece_out, "pair", hop + 1))
        squares = squares + swap(squares, axis, mask)
    back += [swap(sent[mask], "pair", mask) for mask in range(len(hops), pair_count)]
    squares, back = lax.optimization_barrier((squares, back))
    squares = squares + swap(squares, *hops[-1])
    (rotated,) = call(
        functools.partial(place_kernel, rnd=1),
        [plan, table] + back,
        [(piece_rows, ncols)],
        smem=2,
        cost=pl.CostEstimate(flops=0, bytes_accessed=8 * slab.size, transcendentals=0),
    )
    return rotated, jnp.sqrt(squares / total_rows).reshape(ncols)


def solution(mesh):
    specs = (P(("row", "pair"), None), P())
    return jax.shard_map(on_device, mesh=mesh, in_specs=specs, out_specs=specs, check_vma=False)
```

```python
import functools

import jax
import jax.numpy as jnp
from jax import lax
from jax.experimental import pallas as pl
from jax.experimental.pallas import tpu as pltpu
from jax.sharding import PartitionSpec as P

NS_STEPS = 4
PAD = 8
LANES = 128
NOTES = PAIR, KEEPS, NEXT, COMES_FROM = range(4)

VMEM = pl.BlockSpec(memory_space=pltpu.VMEM)
SMEM = pl.BlockSpec(memory_space=pltpu.SMEM)
HBM = pl.BlockSpec(memory_space=pltpu.HBM)
COLS_BY_COLS = (((0,), (0,)), ((), ()))


def split(x):
    high = x.astype(jnp.bfloat16)
    return high, (x - high.astype(jnp.float32)).astype(jnp.bfloat16)


def mul(a, b):
    dot = functools.partial(jnp.dot, preferred_element_type=jnp.float32)
    rows = a[0].shape[0]
    both = dot(jnp.concatenate(a, axis=0), b[0])
    return both[:rows] + (both[rows:] + dot(a[0], b[1]))


def mul_by_cols(a, b):
    dot = functools.partial(lax.dot_general, dimension_numbers=COLS_BY_COLS, preferred_element_type=jnp.float32)
    return dot(a[0], b[0]) + (dot(a[0], b[1]) + dot(a[1], b[0]))


def slot_of(plan_ref, rnd, block, count):
    found = jnp.int32(0)
    for slot in range(1, count):
        found = jnp.where(plan_ref[rnd, slot] == block, slot, found)
    return found


def note(table_ref, kind, device):
    return table_ref[table_ref.shape[0] - len(NOTES) + kind, device]


def sender(table_ref, me):
    return note(table_ref, COMES_FROM, me)


def lay_out(plan_ref, table_ref, rnd):
    rounds, slots = plan_ref.shape
    count = slots // 2
    for row in range(rounds):
        for slot in range(slots):
            table_ref[row, slot] = plan_ref[row, slot]
    pair, half, seen, start = jnp.int32(0), jnp.int32(0), jnp.int32(0), jnp.int32(0)
    for step in range(count):
        device, before = step ^ (step >> 1), (step - 1) ^ ((step - 1) >> 1)
        seen = seen | (jnp.int32(1) << pair)
        table_ref[rounds + PAIR, device] = pair
        table_ref[rounds + KEEPS, device] = half
        table_ref[rounds + NEXT, device] = slot_of(plan_ref, rnd + 1, plan_ref[rnd, 2 * pair + half], slots) // 2
        table_ref[rounds + COMES_FROM, device] = before if step else 0
        table_ref[rounds + COMES_FROM, start] = device
        slot = slot_of(plan_ref, rnd + 1, plan_ref[rnd, 2 * pair + 1 - half], slots)
        joins = slot_of(plan_ref, rnd, plan_ref[rnd + 1, slot ^ 1], slots)
        closed = ((seen >> (joins // 2)) & 1) == 1
        unseen = jnp.int32(0)
        for other in reversed(range(count)):
            unseen = jnp.where(((seen >> other) & 1) == 0, other, unseen)
        pair, half = jnp.where(closed, unseen, joins // 2), jnp.where(closed, 0, joins % 2)
        start = jnp.where(closed, (step + 1) ^ ((step + 1) >> 1), start)


def deal_kernel(plan_hbm, slab_hbm, table_ref, *refs, rnd):
    *outs, plan_ref, slab_ref, plan_sem, slab_sem = refs
    slab_copy = pltpu.make_async_copy(slab_hbm, slab_ref, slab_sem)
    slab_copy.start()
    plan_copy = pltpu.make_async_copy(plan_hbm, plan_ref, plan_sem)
    plan_copy.start()
    plan_copy.wait()
    lay_out(plan_ref, table_ref, rnd)
    slab_copy.wait()
    me = lax.axis_index("pair")
    width = outs[0].shape[1] // 2
    for mask, out in enumerate(outs):
        pair = note(table_ref, PAIR, me ^ mask)
        for half in range(2):
            block = plan_ref[rnd, 2 * pair + half]
            start = pl.multiple_of(block * width, width)
            out[:, half * width : (half + 1) * width] = slab_ref[:, pl.ds(start, width)]


def cross_of(first, second, keep_ref, send_ref, scratch):
    width = first.shape[1]
    scratch[...] = mul_by_cols(split(first), split(second))
    diag = jnp.concatenate(
        [
            jnp.sum(first * first, axis=0, keepdims=True),
            jnp.sum(second * second, axis=0, keepdims=True),
            jnp.zeros((PAD - 2, width), jnp.float32),
        ],
        axis=0,
    )
    core = lax.axis_index("row") & 1
    part = width // 2
    for ref, which in ((keep_ref, core), (send_ref, 1 - core)):
        ref[:part, :] = scratch[pl.ds(pl.multiple_of(which * part, part), part), :]
        ref[part:, :] = diag


def copy_kernel(in_ref, out_ref):
    out_ref[...] = in_ref[...]


def first_cross_kernel(*refs):
    *ins, local_ref, keep_ref, send_ref, scratch = refs
    me = lax.axis_index("pair")
    rows = ins[0].shape[0]
    width = ins[0].shape[1] // 2
    for mask, ref in enumerate(ins):
        local_ref[pl.ds(pl.multiple_of((me ^ mask) * rows, rows), rows), :] = ref[...]
    cross_of(local_ref[:, :width], local_ref[:, width:], keep_ref, send_ref, scratch)


def coupling_of(mine, other):
    part = mine.shape[0] - PAD
    upper = (lax.axis_index("row") & 1) == 0
    cross = jnp.concatenate(
        [jnp.where(upper, mine[:part], other[:part]), jnp.where(upper, other[:part], mine[:part])], axis=0
    )
    diag_first = jnp.transpose(mine[part:])[:, :1]
    diag_second = mine[part + 1 : part + 2]
    coupling = cross / (diag_first + diag_second + 1e-06)
    return coupling, jnp.transpose(coupling)


def turned(sides):
    width = sides[0][0].shape[0]
    ident = lax.broadcasted_iota(jnp.int32, (width, width), 0) == lax.broadcasted_iota(jnp.int32, (width, width), 1)
    scales, squares, blocks = [], [], []
    for k, kt, block, sign, partner in sides:
        inv_sq = 1.0 / (1.0 + jnp.sum(k * k))
        product = mul(split(jnp.concatenate([k, partner], axis=0)), split(kt))
        square = product[:width]
        squares.append(jnp.where(ident, square + 1.0, square) * inv_sq)
        blocks.append(block + sign * product[width:])
        scales.append(jnp.sqrt(inv_sq))
    for step in range(NS_STEPS):
        moves = []
        for square in squares:
            half = -0.5 * square
            moves.append(split(jnp.where(ident, half + 1.5, half)))
        if step < NS_STEPS - 1:
            products = [
                mul(split(jnp.concatenate([square, block], axis=0)), move)
                for square, block, move in zip(squares, blocks, moves)
            ]
            squares = [mul(split(product[:width]), move) for product, move in zip(products, moves)]
            blocks = [product[width:] for product in products]
        else:
            blocks = [mul(split(block), move) for block, move in zip(blocks, moves)]
    return [block * scale for block, scale in zip(blocks, scales)]


def half_of(ref, half):
    width = ref.shape[1] // 2
    return ref[:, pl.ds(pl.multiple_of(half * width, width), width)]


def turn_kernel(table_ref, mine_ref, other_ref, local_ref, *refs, rnd, masks):
    came_refs, came_other_refs, raw_refs = (refs[i * len(masks) : (i + 1) * len(masks)] for i in range(3))
    outs = refs[3 * len(masks) :]
    next_ref, keep_ref, send_ref, scratch = outs
    me = lax.axis_index("pair")
    kept = note(table_ref, KEEPS, me)
    gets = 1 - note(table_ref, KEEPS, sender(table_ref, me))
    source = sender(table_ref, me)

    def pick(parts):
        picked = parts[0]
        for mask, part in zip(masks[1:], parts[1:]):
            picked = jnp.where(source == (me ^ mask), part, picked)
        return picked

    sides = []
    for half, mine, other, halves in (
        (kept, mine_ref[...], other_ref[...], [half_of(local_ref, kept), half_of(local_ref, 1 - kept)]),
        (
            gets,
            pick([ref[...] for ref in came_refs]),
            pick([ref[...] for ref in came_other_refs]),
            [pick([half_of(ref, half) for ref in raw_refs]) for half in (gets, 1 - gets)],
        ),
    ):
        k, kt = coupling_of(mine, other)
        is_first = half == 0
        sides.append(
            (
                jnp.where(is_first, k, kt),
                jnp.where(is_first, kt, k),
                halves[0],
                jnp.where(is_first, -1.0, 1.0),
                halves[1],
            )
        )
    new = turned(sides)
    kept_first = table_ref[rnd, 2 * note(table_ref, PAIR, me) + kept] == table_ref[rnd + 1, 2 * note(table_ref, NEXT, me)]
    first = jnp.where(kept_first, new[0], new[1])
    second = jnp.where(kept_first, new[1], new[0])
    width = first.shape[1]
    next_ref[:, :width] = first
    next_ref[:, width:] = second
    cross_of(first, second, keep_ref, send_ref, scratch)


def last_turn_kernel(table_ref, mine_ref, other_ref, local_ref, *refs, rnd):
    *outs, squares_ref, scratch = refs
    width = local_ref.shape[1] // 2
    first, second = local_ref[:, :width], local_ref[:, width:]
    k, kt = coupling_of(mine_ref[...], other_ref[...])
    new = turned([(k, kt, first, -1.0, second), (kt, k, second, 1.0, first)])
    me = lax.axis_index("pair")
    squares_ref[...] = jnp.zeros_like(squares_ref)
    for half in range(2):
        scratch[:, half * width : (half + 1) * width] = new[half]
        block = table_ref[rnd, 2 * note(table_ref, NEXT, me) + half]
        sums = jnp.sum(new[half] * new[half], axis=0, keepdims=True)
        for lane in range(0, width, LANES):
            squares_ref[pl.ds((block * width + lane) // LANES, 1), :] = sums[:, lane : lane + LANES]
    rows = outs[0].shape[0]
    for mask, out in enumerate(outs):
        out[...] = scratch[pl.ds(pl.multiple_of((me ^ mask) * rows, rows), rows), :]


def place_kernel(table_ref, *refs, rnd):
    *ins, out_ref = refs
    width = ins[0].shape[1] // 2
    me = lax.axis_index("pair")
    for mask, ref in enumerate(ins):
        for half in range(2):
            block = table_ref[rnd, 2 * note(table_ref, NEXT, me ^ mask) + half]
            start = pl.multiple_of(block * width, width)
            out_ref[:, pl.ds(start, width)] = ref[:, half * width : (half + 1) * width]


def swap(x, axis, mask):
    return lax.ppermute(x, axis, [(i, i ^ mask) for i in range(lax.axis_size(axis))])


def spread(parts):
    return [parts[0]] + [swap(parts[mask], "pair", mask) for mask in range(1, len(parts))]


def tree_sum(parts):
    while len(parts) > 1:
        parts = [a + b for a, b in zip(parts[::2], parts[1::2])]
    return parts[0]


def over_chips(x):
    return tree_sum([x] + [swap(x, "row", mask) for mask in range(2, lax.axis_size("row"), 2)])


def powers(size):
    return [1 << bit for bit in range(size.bit_length() - 1)]


def call(kernel, ins, outs, scratch=(), table=None, cost=None):
    ins = ([] if table is None else [table]) + ins
    return pl.pallas_call(
        kernel,
        out_shape=[jax.ShapeDtypeStruct(shape, jnp.float32) for shape in outs],
        in_specs=[SMEM] * (table is not None) + [VMEM] * (len(ins) - (table is not None)),
        out_specs=[VMEM] * len(outs),
        scratch_shapes=[pltpu.VMEM(shape, jnp.float32) for shape in scratch],
        compiler_params=pltpu.CompilerParams(vmem_limit_bytes=24 * 2**20),
        cost_estimate=cost,
    )(*ins)


def deal(plan, slab, rnd):
    piece_rows, ncols = slab.shape
    rounds, blocks = plan.shape
    pieces = [jax.ShapeDtypeStruct((piece_rows, 2 * ncols // blocks), jnp.float32)] * (blocks // 2)
    table, *pieces = pl.pallas_call(
        functools.partial(deal_kernel, rnd=rnd),
        out_shape=[jax.ShapeDtypeStruct((rounds + len(NOTES), blocks), jnp.int32)] + pieces,
        in_specs=[HBM, HBM],
        out_specs=[SMEM] + [VMEM] * len(pieces),
        scratch_shapes=[
            pltpu.SMEM(plan.shape, jnp.int32),
            pltpu.VMEM(slab.shape, jnp.float32),
            pltpu.SemaphoreType.DMA,
            pltpu.SemaphoreType.DMA,
        ],
        compiler_params=pltpu.CompilerParams(vmem_limit_bytes=58 * 2**20),
    )(plan, slab)
    return table, pieces


def on_device(slab, plan):
    piece_rows, ncols = slab.shape
    pair_count = lax.axis_size("pair")
    both = ncols // pair_count
    width = both // 2
    group_rows = piece_rows * pair_count
    total_rows = group_rows * lax.axis_size("row")
    crossed = [(group_rows, both), (width // 2 + PAD, width), (width // 2 + PAD, width)]
    square = (width, width)
    masks = powers(pair_count) if pair_count <= 4 else list(range(1, pair_count))

    table, dealt = deal(plan, slab, 0)
    own, *others = spread(dealt)
    own = call(copy_kernel, [own], [own.shape])
    local, keep, send = call(first_cross_kernel, [*own, *others], crossed, [square])
    raw = [swap(local, "pair", mask) for mask in masks]
    mine = over_chips(keep + swap(send, "row", 1))
    came = [swap(mine, "pair", mask) for mask in masks]
    came_other = [swap(x, "row", 1) for x in came]
    local, keep, send = call(
        functools.partial(turn_kernel, rnd=0, masks=masks),
        [mine, swap(mine, "row", 1), local] + came + came_other + raw,
        crossed,
        [square],
        table,
    )
    mine = over_chips(keep + swap(send, "row", 1))
    *sent, squares = call(
        functools.partial(last_turn_kernel, rnd=1),
        [mine, swap(mine, "row", 1), local],
        [(piece_rows, both)] * pair_count + [(ncols // LANES, LANES)],
        [(group_rows, both)],
        table,
    )
    back = spread(sent)
    squares = over_chips(squares + swap(squares, "row", 1))
    hops = powers(pair_count)
    for mask in hops[:-1]:
        squares = squares + swap(squares, "pair", mask)
    squares, back = lax.optimization_barrier((squares, back))
    squares = squares + swap(squares, "pair", hops[-1])
    (rotated,) = call(
        functools.partial(place_kernel, rnd=1),
        back,
        [(piece_rows, ncols)],
        table=table,
        cost=pl.CostEstimate(flops=0, bytes_accessed=8 * slab.size, transcendentals=0),
    )
    return rotated, jnp.sqrt(squares / total_rows).reshape(ncols)


def solution(mesh):
    specs = (P(("row", "pair"), None), P())
    return jax.shard_map(on_device, mesh=mesh, in_specs=specs, out_specs=specs, check_vma=False)
```

```python
import functools

import jax
import jax.numpy as jnp
from jax import lax
from jax.experimental import pallas as pl
from jax.experimental.pallas import tpu as pltpu
from jax.sharding import PartitionSpec as P

NS_STEPS = 4
PAD = 8
LANES = 128
NOTES = PAIR, KEEPS, NEXT, COMES_FROM = range(4)

VMEM = pl.BlockSpec(memory_space=pltpu.VMEM)
SMEM = pl.BlockSpec(memory_space=pltpu.SMEM)
HBM = pl.BlockSpec(memory_space=pltpu.HBM)
COLS_BY_COLS = (((0,), (0,)), ((), ()))


def split(x):
    high = x.astype(jnp.bfloat16)
    return high, (x - high.astype(jnp.float32)).astype(jnp.bfloat16)


def mul(a, b):
    dot = functools.partial(jnp.dot, preferred_element_type=jnp.float32)
    rows = a[0].shape[0]
    both = dot(jnp.concatenate(a, axis=0), b[0])
    return both[:rows] + (both[rows:] + dot(a[0], b[1]))


def mul_by_cols(a, b):
    dot = functools.partial(lax.dot_general, dimension_numbers=COLS_BY_COLS, preferred_element_type=jnp.float32)
    return dot(a[0], b[0]) + (dot(a[0], b[1]) + dot(a[1], b[0]))


def slot_of(plan_ref, rnd, block, count):
    found = jnp.int32(0)
    for slot in range(1, count):
        found = jnp.where(plan_ref[rnd, slot] == block, slot, found)
    return found


def note(table_ref, kind, device):
    return table_ref[table_ref.shape[0] - len(NOTES) + kind, device]


def sender(table_ref, me):
    return note(table_ref, COMES_FROM, me)


def lay_out(plan_ref, table_ref, rnd):
    rounds, slots = plan_ref.shape
    count = slots // 2
    for row in range(rounds):
        for slot in range(slots):
            table_ref[row, slot] = plan_ref[row, slot]
    pair, half, seen, start = jnp.int32(0), jnp.int32(0), jnp.int32(0), jnp.int32(0)
    for step in range(count):
        device, before = step ^ (step >> 1), (step - 1) ^ ((step - 1) >> 1)
        seen = seen | (jnp.int32(1) << pair)
        table_ref[rounds + PAIR, device] = pair
        table_ref[rounds + KEEPS, device] = half
        table_ref[rounds + NEXT, device] = slot_of(plan_ref, rnd + 1, plan_ref[rnd, 2 * pair + half], slots) // 2
        table_ref[rounds + COMES_FROM, device] = before if step else 0
        table_ref[rounds + COMES_FROM, start] = device
        slot = slot_of(plan_ref, rnd + 1, plan_ref[rnd, 2 * pair + 1 - half], slots)
        joins = slot_of(plan_ref, rnd, plan_ref[rnd + 1, slot ^ 1], slots)
        closed = ((seen >> (joins // 2)) & 1) == 1
        unseen = jnp.int32(0)
        for other in reversed(range(count)):
            unseen = jnp.where(((seen >> other) & 1) == 0, other, unseen)
        pair, half = jnp.where(closed, unseen, joins // 2), jnp.where(closed, 0, joins % 2)
        start = jnp.where(closed, (step + 1) ^ ((step + 1) >> 1), start)


def deal_piece(table_ref, slab_ref, out, rnd, device):
    width = out.shape[1] // 2
    for half in range(2):
        block = table_ref[rnd, 2 * note(table_ref, PAIR, device) + half]
        start = pl.multiple_of(block * width, width)
        out[: slab_ref.shape[0], half * width : (half + 1) * width] = slab_ref[:, pl.ds(start, width)]


def deal_kernel(plan_hbm, slab_hbm, table_ref, *refs, rnd):
    *outs, plan_ref, slab_ref, plan_sem, slab_sem = refs
    slab_copy = pltpu.make_async_copy(slab_hbm, slab_ref, slab_sem)
    slab_copy.start()
    plan_copy = pltpu.make_async_copy(plan_hbm, plan_ref, plan_sem)
    plan_copy.start()
    plan_copy.wait()
    lay_out(plan_ref, table_ref, rnd)
    slab_copy.wait()
    me = lax.axis_index("pair")
    for mask, out in enumerate(outs):
        deal_piece(table_ref, slab_ref, out, rnd, me ^ mask)


def parts_of(width):
    lanes = width // LANES
    return (lanes * width // 2 + -(-2 * lanes // PAD) * PAD, LANES)


def cross_of(first, second, keep_ref, send_ref, scratch):
    width = first.shape[1]
    scratch[...] = mul_by_cols(split(first), split(second))
    sums = [jnp.sum(block * block, axis=0, keepdims=True) for block in (first, second)]
    core = lax.axis_index("row") & 1
    part, lanes = width // 2, width // LANES
    for ref, which in ((keep_ref, core), (send_ref, 1 - core)):
        rows = pl.ds(pl.multiple_of(which * part, part), part)
        for lane in range(lanes):
            columns = slice(lane * LANES, (lane + 1) * LANES)
            ref[lane * part : (lane + 1) * part, :] = scratch[rows, columns]
            for block in range(2):
                row = lanes * part + block * lanes + lane
                ref[row : row + 1, :] = sums[block][:, columns]
        filled = lanes * (part + 2)
        ref[filled:, :] = jnp.zeros((ref.shape[0] - filled, LANES), jnp.float32)


def copy_kernel(in_ref, out_ref):
    out_ref[...] = in_ref[...]


def first_cross_kernel(*refs):
    *ins, local_ref, keep_ref, send_ref, scratch = refs
    me = lax.axis_index("pair")
    rows = ins[0].shape[0]
    width = ins[0].shape[1] // 2
    for mask, ref in enumerate(ins):
        local_ref[pl.ds(pl.multiple_of((me ^ mask) * rows, rows), rows), :] = ref[...]
    cross_of(local_ref[:, :width], local_ref[:, width:], keep_ref, send_ref, scratch)


def coupling_of(mine, other, width):
    part, lanes = width // 2, width // LANES
    upper = (lax.axis_index("row") & 1) == 0
    halves = [
        jnp.concatenate([half[lane * part : (lane + 1) * part] for lane in range(lanes)], axis=1)
        for half in (mine, other)
    ]
    cross = jnp.concatenate(
        [jnp.where(upper, halves[0], halves[1]), jnp.where(upper, halves[1], halves[0])], axis=0
    )
    sums = mine[lanes * part :]
    diag_first = jnp.concatenate([jnp.transpose(sums)[:, lane : lane + 1] for lane in range(lanes)], axis=0)
    diag_second = jnp.concatenate([sums[lanes + lane : lanes + lane + 1] for lane in range(lanes)], axis=1)
    coupling = cross / (diag_first + diag_second + 1e-06)
    return coupling, jnp.transpose(coupling)


def turned(sides):
    width = sides[0][0].shape[0]
    ident = lax.broadcasted_iota(jnp.int32, (width, width), 0) == lax.broadcasted_iota(jnp.int32, (width, width), 1)
    scales, squares, blocks = [], [], []
    for k, kt, block, sign, partner in sides:
        inv_sq = 1.0 / (1.0 + jnp.sum(k * k))
        product = mul(split(jnp.concatenate([k, partner], axis=0)), split(kt))
        square = product[:width]
        squares.append(jnp.where(ident, square + 1.0, square) * inv_sq)
        blocks.append(block + sign * product[width:])
        scales.append(jnp.sqrt(inv_sq))
    for step in range(NS_STEPS):
        moves = []
        for square in squares:
            half = -0.5 * square
            moves.append(split(jnp.where(ident, half + 1.5, half)))
        if step < NS_STEPS - 1:
            products = [
                mul(split(jnp.concatenate([square, block], axis=0)), move)
                for square, block, move in zip(squares, blocks, moves)
            ]
            squares = [mul(split(product[:width]), move) for product, move in zip(products, moves)]
            blocks = [product[width:] for product in products]
        else:
            blocks = [mul(split(block), move) for block, move in zip(blocks, moves)]
    return [block * scale for block, scale in zip(blocks, scales)]


def half_of(ref, half):
    width = ref.shape[1] // 2
    return ref[:, pl.ds(pl.multiple_of(half * width, width), width)]


def ahead_kernel(table_ref, slab_ref, local_ref, own_ref, *outs, rnd, masks, rest):
    me = lax.axis_index("pair")
    rows = own_ref.shape[0]
    for mask, out in zip([0, *masks], [own_ref, *outs]):
        device = me ^ mask
        deal_piece(table_ref, slab_ref, out, rnd, sender(table_ref, device))
        if mask:
            for index, other in enumerate(rest):
                start = pl.multiple_of((device ^ other) * rows, rows)
                out[(index + 1) * rows : (index + 2) * rows, :] = local_ref[pl.ds(start, rows), :]


def one_side(mine, other, ref, half):
    k, kt = coupling_of(mine, other, ref.shape[1] // 2)
    is_first = half == 0
    return (
        jnp.where(is_first, k, kt),
        jnp.where(is_first, kt, k),
        half_of(ref, half),
        jnp.where(is_first, -1.0, 1.0),
        half_of(ref, 1 - half),
    )


def turn_kernel(table_ref, mine_ref, other_ref, local_ref, own_ref, *refs, rnd, masks, rest):
    *refs, next_ref, keep_ref, send_ref, scratch, raw_ref = refs
    came_refs, came_other_refs, raw_refs = (refs[i * len(masks) : (i + 1) * len(masks)] for i in range(3))
    me = lax.axis_index("pair")
    source = sender(table_ref, me)
    rows = own_ref.shape[0]

    def pick(parts):
        picked = parts[0]
        for mask, part in zip(masks[1:], parts[1:]):
            picked = jnp.where(source == (me ^ mask), part, picked)
        return picked

    def put(other, piece):
        raw_ref[pl.ds(pl.multiple_of((me ^ other) * rows, rows), rows), :] = piece

    put(0, own_ref[...])
    for mask, ref in zip(masks, raw_refs):
        put(mask, ref[:rows, :])
    for index, other in enumerate(rest):
        put(other, pick([ref[(index + 1) * rows : (index + 2) * rows, :] for ref in raw_refs]))
    half = 1 - note(table_ref, KEEPS, source)
    came_pair = pick([ref[...] for ref in came_refs]), pick([ref[...] for ref in came_other_refs])
    kept, came = turned(
        [
            one_side(mine_ref[...], other_ref[...], local_ref, note(table_ref, KEEPS, me)),
            one_side(*came_pair, raw_ref, half),
        ]
    )
    kept_block = table_ref[rnd, 2 * note(table_ref, PAIR, me) + note(table_ref, KEEPS, me)]
    kept_first = kept_block == table_ref[rnd + 1, 2 * note(table_ref, NEXT, me)]
    first, second = jnp.where(kept_first, kept, came), jnp.where(kept_first, came, kept)
    width = first.shape[1]
    next_ref[:, :width] = first
    next_ref[:, width:] = second
    cross_of(first, second, keep_ref, send_ref, scratch)


def last_turn_kernel(table_ref, mine_ref, other_ref, local_ref, *refs, rnd):
    *outs, squares_ref, scratch = refs
    width = local_ref.shape[1] // 2
    first, second = local_ref[:, :width], local_ref[:, width:]
    k, kt = coupling_of(mine_ref[...], other_ref[...], width)
    new = turned([(k, kt, first, -1.0, second), (kt, k, second, 1.0, first)])
    me = lax.axis_index("pair")
    squares_ref[...] = jnp.zeros_like(squares_ref)
    for half in range(2):
        scratch[:, half * width : (half + 1) * width] = new[half]
        block = table_ref[rnd, 2 * note(table_ref, NEXT, me) + half]
        sums = jnp.sum(new[half] * new[half], axis=0, keepdims=True)
        for lane in range(0, width, LANES):
            squares_ref[pl.ds((block * width + lane) // LANES, 1), :] = sums[:, lane : lane + LANES]
    rows = outs[0].shape[0]
    for mask, out in enumerate(outs):
        out[...] = scratch[pl.ds(pl.multiple_of((me ^ mask) * rows, rows), rows), :]


def place_kernel(table_ref, *refs, rnd):
    *ins, out_ref = refs
    width = ins[0].shape[1] // 2
    me = lax.axis_index("pair")
    for mask, ref in enumerate(ins):
        for half in range(2):
            block = table_ref[rnd, 2 * note(table_ref, NEXT, me ^ mask) + half]
            start = pl.multiple_of(block * width, width)
            out_ref[:, pl.ds(start, width)] = ref[:, half * width : (half + 1) * width]


def swap(x, axis, mask):
    return lax.ppermute(x, axis, [(i, i ^ mask) for i in range(lax.axis_size(axis))])


def spread(parts):
    return [parts[0]] + [swap(parts[mask], "pair", mask) for mask in range(1, len(parts))]


def tree_sum(parts):
    while len(parts) > 1:
        parts = [a + b for a, b in zip(parts[::2], parts[1::2])]
    return parts[0]


def over_chips(x):
    return tree_sum([x] + [swap(x, "row", mask) for mask in range(2, lax.axis_size("row"), 2)])


def powers(size):
    return [1 << bit for bit in range(size.bit_length() - 1)]


def call(kernel, ins, outs, scratch=(), table=None, cost=None):
    ins = ([] if table is None else [table]) + ins
    return pl.pallas_call(
        kernel,
        out_shape=[jax.ShapeDtypeStruct(shape, jnp.float32) for shape in outs],
        in_specs=[SMEM] * (table is not None) + [VMEM] * (len(ins) - (table is not None)),
        out_specs=[VMEM] * len(outs),
        scratch_shapes=[pltpu.VMEM(shape, jnp.float32) for shape in scratch],
        compiler_params=pltpu.CompilerParams(vmem_limit_bytes=24 * 2**20),
        cost_estimate=cost,
    )(*ins)


def deal(plan, slab, rnd):
    piece_rows, ncols = slab.shape
    rounds, blocks = plan.shape
    pieces = [jax.ShapeDtypeStruct((piece_rows, 2 * ncols // blocks), jnp.float32)] * (blocks // 2)
    table, *pieces = pl.pallas_call(
        functools.partial(deal_kernel, rnd=rnd),
        out_shape=[jax.ShapeDtypeStruct((rounds + len(NOTES), blocks), jnp.int32)] + pieces,
        in_specs=[HBM, HBM],
        out_specs=[SMEM] + [VMEM] * len(pieces),
        scratch_shapes=[
            pltpu.SMEM(plan.shape, jnp.int32),
            pltpu.VMEM(slab.shape, jnp.float32),
            pltpu.SemaphoreType.DMA,
            pltpu.SemaphoreType.DMA,
        ],
        compiler_params=pltpu.CompilerParams(vmem_limit_bytes=58 * 2**20),
    )(plan, slab)
    return table, pieces


def on_device(slab, plan):
    piece_rows, ncols = slab.shape
    pair_count = lax.axis_size("pair")
    both = ncols // pair_count
    width = both // 2
    group_rows = piece_rows * pair_count
    total_rows = group_rows * lax.axis_size("row")
    crossed = [(group_rows, both), parts_of(width), parts_of(width)]
    square = (width, width)
    masks = powers(pair_count) if pair_count <= 4 else list(range(1, pair_count))
    rest = [mask for mask in range(1, pair_count) if mask not in masks]

    table, dealt = deal(plan, slab, 0)
    own, *others = spread(dealt)
    own = call(copy_kernel, [own], [own.shape])
    local, keep, send = call(first_cross_kernel, [*own, *others], crossed, [square])
    own, *ahead = call(
        functools.partial(ahead_kernel, rnd=0, masks=masks, rest=rest),
        [slab, local],
        [(piece_rows, both)] + [((1 + len(rest)) * piece_rows, both)] * len(masks),
        table=table,
    )
    total, ahead = lax.optimization_barrier((keep + swap(send, "row", 1), ahead))
    raw = [swap(x, "pair", mask) for x, mask in zip(ahead, masks)]
    mine, raw = lax.optimization_barrier((over_chips(total), raw))
    came = [swap(mine, "pair", mask) for mask in masks]
    came_other = [swap(x, "row", 1) for x in came]
    local, keep, send = call(
        functools.partial(turn_kernel, rnd=0, masks=masks, rest=rest),
        [mine, swap(mine, "row", 1), local, own] + came + came_other + raw,
        crossed,
        [square, (group_rows, both)],
        table,
    )
    mine = over_chips(keep + swap(send, "row", 1))
    *sent, squares = call(
        functools.partial(last_turn_kernel, rnd=1),
        [mine, swap(mine, "row", 1), local],
        [(piece_rows, both)] * pair_count + [(ncols // LANES, LANES)],
        [(group_rows, both)],
        table,
    )
    back = spread(sent)
    squares = over_chips(squares + swap(squares, "row", 1))
    hops = powers(pair_count)
    for mask in hops[:-1]:
        squares = squares + swap(squares, "pair", mask)
    squares, back = lax.optimization_barrier((squares, back))
    squares = squares + swap(squares, "pair", hops[-1])
    (rotated,) = call(
        functools.partial(place_kernel, rnd=1),
        back,
        [(piece_rows, ncols)],
        table=table,
        cost=pl.CostEstimate(flops=0, bytes_accessed=8 * slab.size, transcendentals=0),
    )
    return rotated, jnp.sqrt(squares / total_rows).reshape(ncols)


def solution(mesh):
    specs = (P(("row", "pair"), None), P())
    return jax.shard_map(on_device, mesh=mesh, in_specs=specs, out_specs=specs, check_vma=False)
```

```python
import functools

import jax
import jax.numpy as jnp
from jax import lax
from jax.experimental import pallas as pl
from jax.experimental.pallas import tpu as pltpu
from jax.sharding import PartitionSpec as P

NS_STEPS = 4
PAD = 8
LANES = 128
NOTES = PAIR, KEEPS, NEXT, COMES_FROM = range(4)

VMEM = pl.BlockSpec(memory_space=pltpu.VMEM)
SMEM = pl.BlockSpec(memory_space=pltpu.SMEM)
HBM = pl.BlockSpec(memory_space=pltpu.HBM)
COLS_BY_COLS = (((0,), (0,)), ((), ()))


def split(x):
    high = x.astype(jnp.bfloat16)
    return high, (x - high.astype(jnp.float32)).astype(jnp.bfloat16)


def mul(a, b):
    dot = functools.partial(jnp.dot, preferred_element_type=jnp.float32)
    rows = a[0].shape[0]
    both = dot(jnp.concatenate(a, axis=0), b[0])
    return both[:rows] + (both[rows:] + dot(a[0], b[1]))


def mul_by_cols(a, b):
    dot = functools.partial(lax.dot_general, dimension_numbers=COLS_BY_COLS, preferred_element_type=jnp.float32)
    return dot(a[0], b[0]) + (dot(a[0], b[1]) + dot(a[1], b[0]))


def slot_of(plan_ref, rnd, block, count):
    found = jnp.int32(0)
    for slot in range(1, count):
        found = jnp.where(plan_ref[rnd, slot] == block, slot, found)
    return found


def note(table_ref, kind, device):
    return table_ref[table_ref.shape[0] - len(NOTES) + kind, device]


def sender(table_ref, me):
    return note(table_ref, COMES_FROM, me)


def lay_out(plan_ref, table_ref, rnd):
    rounds, slots = plan_ref.shape
    count = slots // 2
    for row in range(rounds):
        for slot in range(slots):
            table_ref[row, slot] = plan_ref[row, slot]
    pair, half, seen, start = jnp.int32(0), jnp.int32(0), jnp.int32(0), jnp.int32(0)
    for step in range(count):
        device, before = step ^ (step >> 1), (step - 1) ^ ((step - 1) >> 1)
        seen = seen | (jnp.int32(1) << pair)
        table_ref[rounds + PAIR, device] = pair
        table_ref[rounds + KEEPS, device] = half
        table_ref[rounds + NEXT, device] = slot_of(plan_ref, rnd + 1, plan_ref[rnd, 2 * pair + half], slots) // 2
        table_ref[rounds + COMES_FROM, device] = before if step else 0
        table_ref[rounds + COMES_FROM, start] = device
        slot = slot_of(plan_ref, rnd + 1, plan_ref[rnd, 2 * pair + 1 - half], slots)
        joins = slot_of(plan_ref, rnd, plan_ref[rnd + 1, slot ^ 1], slots)
        closed = ((seen >> (joins // 2)) & 1) == 1
        unseen = jnp.int32(0)
        for other in reversed(range(count)):
            unseen = jnp.where(((seen >> other) & 1) == 0, other, unseen)
        pair, half = jnp.where(closed, unseen, joins // 2), jnp.where(closed, 0, joins % 2)
        start = jnp.where(closed, (step + 1) ^ ((step + 1) >> 1), start)


def deal_piece(table_ref, slab_ref, out, rnd, device):
    width = out.shape[1] // 2
    for half in range(2):
        block = table_ref[rnd, 2 * note(table_ref, PAIR, device) + half]
        start = pl.multiple_of(block * width, width)
        out[: slab_ref.shape[0], half * width : (half + 1) * width] = slab_ref[:, pl.ds(start, width)]


def deal_kernel(plan_hbm, slab_hbm, table_ref, *refs, rnd):
    *outs, plan_ref, slab_ref, plan_sem, slab_sem = refs
    slab_copy = pltpu.make_async_copy(slab_hbm, slab_ref, slab_sem)
    slab_copy.start()
    plan_copy = pltpu.make_async_copy(plan_hbm, plan_ref, plan_sem)
    plan_copy.start()
    plan_copy.wait()
    lay_out(plan_ref, table_ref, rnd)
    slab_copy.wait()
    me = lax.axis_index("pair")
    for mask, out in enumerate(outs):
        deal_piece(table_ref, slab_ref, out, rnd, me ^ mask)


def parts_of(width):
    lanes = width // LANES
    return (lanes * width // 2 + -(-2 * lanes // PAD) * PAD, LANES)


def cross_of(first, second, keep_ref, send_ref, scratch):
    width = first.shape[1]
    scratch[...] = mul_by_cols(split(first), split(second))
    sums = [jnp.sum(block * block, axis=0, keepdims=True) for block in (first, second)]
    core = lax.axis_index("row") & 1
    part, lanes = width // 2, width // LANES
    for ref, which in ((keep_ref, core), (send_ref, 1 - core)):
        rows = pl.ds(pl.multiple_of(which * part, part), part)
        for lane in range(lanes):
            columns = slice(lane * LANES, (lane + 1) * LANES)
            ref[lane * part : (lane + 1) * part, :] = scratch[rows, columns]
            for block in range(2):
                row = lanes * part + block * lanes + lane
                ref[row : row + 1, :] = sums[block][:, columns]
        filled = lanes * (part + 2)
        ref[filled:, :] = jnp.zeros((ref.shape[0] - filled, LANES), jnp.float32)


def copy_kernel(in_ref, out_ref):
    out_ref[...] = in_ref[...]


def first_cross_kernel(*refs):
    *ins, local_ref, keep_ref, send_ref, scratch = refs
    me = lax.axis_index("pair")
    rows = ins[0].shape[0]
    width = ins[0].shape[1] // 2
    for mask, ref in enumerate(ins):
        local_ref[pl.ds(pl.multiple_of((me ^ mask) * rows, rows), rows), :] = ref[...]
    cross_of(local_ref[:, :width], local_ref[:, width:], keep_ref, send_ref, scratch)


def coupling_of(mine, other, width):
    part, lanes = width // 2, width // LANES
    upper = (lax.axis_index("row") & 1) == 0
    halves = [
        jnp.concatenate([half[lane * part : (lane + 1) * part] for lane in range(lanes)], axis=1)
        for half in (mine, other)
    ]
    cross = jnp.concatenate(
        [jnp.where(upper, halves[0], halves[1]), jnp.where(upper, halves[1], halves[0])], axis=0
    )
    sums = mine[lanes * part :]
    diag_first = jnp.concatenate([jnp.transpose(sums)[:, lane : lane + 1] for lane in range(lanes)], axis=0)
    diag_second = jnp.concatenate([sums[lanes + lane : lanes + lane + 1] for lane in range(lanes)], axis=1)
    coupling = cross / (diag_first + diag_second + 1e-06)
    return coupling, jnp.transpose(coupling)


def turned(sides):
    width = sides[0][0].shape[0]
    ident = lax.broadcasted_iota(jnp.int32, (width, width), 0) == lax.broadcasted_iota(jnp.int32, (width, width), 1)
    scales, squares, blocks = [], [], []
    for k, kt, block, sign, partner in sides:
        inv_sq = 1.0 / (1.0 + jnp.sum(k * k))
        product = mul(split(jnp.concatenate([k, partner], axis=0)), split(kt))
        square = product[:width]
        squares.append(jnp.where(ident, square + 1.0, square) * inv_sq)
        blocks.append(block + sign * product[width:])
        scales.append(jnp.sqrt(inv_sq))
    for step in range(NS_STEPS):
        moves = []
        for square in squares:
            half = -0.5 * square
            moves.append(split(jnp.where(ident, half + 1.5, half)))
        if step < NS_STEPS - 1:
            upper = [mul(split(square[: width // 2]), move) for square, move in zip(squares, moves)]
            lower = [mul(split(square[width // 2 :]), move) for square, move in zip(squares, moves)]
            upper = [mul(split(square), move) for square, move in zip(upper, moves)]
            lower = [mul(split(square), move) for square, move in zip(lower, moves)]
            squares = [jnp.concatenate(halves, axis=0) for halves in zip(upper, lower)]
        blocks = [mul(split(block), move) for block, move in zip(blocks, moves)]
    return [block * scale for block, scale in zip(blocks, scales)]


def half_of(ref, half):
    width = ref.shape[1] // 2
    return ref[:, pl.ds(pl.multiple_of(half * width, width), width)]


def ahead_kernel(table_ref, slab_ref, local_ref, own_ref, *outs, rnd, masks, rest):
    me = lax.axis_index("pair")
    rows = own_ref.shape[0]
    for mask, out in zip([0, *masks], [own_ref, *outs]):
        device = me ^ mask
        deal_piece(table_ref, slab_ref, out, rnd, sender(table_ref, device))
        if mask:
            for index, other in enumerate(rest):
                start = pl.multiple_of((device ^ other) * rows, rows)
                out[(index + 1) * rows : (index + 2) * rows, :] = local_ref[pl.ds(start, rows), :]


def one_side(pair_coupling, ref, half):
    k, kt = pair_coupling
    is_first = half == 0
    return (
        jnp.where(is_first, k, kt),
        jnp.where(is_first, kt, k),
        half_of(ref, half),
        jnp.where(is_first, -1.0, 1.0),
        half_of(ref, 1 - half),
    )


def turn_kernel(get_table, mine_ref, other_ref, local_ref, own_ref, *refs, rnd, masks, rest):
    *refs, next_ref, keep_ref, send_ref, scratch, raw_ref = refs
    came_refs, came_other_refs, raw_refs = (refs[i * len(masks) : (i + 1) * len(masks)] for i in range(3))
    me = lax.axis_index("pair")
    rows, width = own_ref.shape[0], own_ref.shape[1] // 2

    def put(other, piece):
        raw_ref[pl.ds(pl.multiple_of((me ^ other) * rows, rows), rows), :] = piece

    put(0, own_ref[...])
    for mask, ref in zip(masks, raw_refs):
        put(mask, ref[:rows, :])
    coupling = coupling_of(mine_ref[...], other_ref[...], width)
    table_ref = get_table()
    source = sender(table_ref, me)

    def pick(parts):
        picked = parts[0]
        for mask, part in zip(masks[1:], parts[1:]):
            picked = jnp.where(source == (me ^ mask), part, picked)
        return picked

    for index, other in enumerate(rest):
        put(other, pick([ref[(index + 1) * rows : (index + 2) * rows, :] for ref in raw_refs]))
    came_coupling = coupling_of(
        pick([ref[...] for ref in came_refs]), pick([ref[...] for ref in came_other_refs]), width
    )
    kept, came = turned(
        [
            one_side(coupling, local_ref, note(table_ref, KEEPS, me)),
            one_side(came_coupling, raw_ref, 1 - note(table_ref, KEEPS, source)),
        ]
    )
    kept_block = table_ref[rnd, 2 * note(table_ref, PAIR, me) + note(table_ref, KEEPS, me)]
    kept_first = kept_block == table_ref[rnd + 1, 2 * note(table_ref, NEXT, me)]
    first, second = jnp.where(kept_first, kept, came), jnp.where(kept_first, came, kept)
    next_ref[:, :width] = first
    next_ref[:, width:] = second
    cross_of(first, second, keep_ref, send_ref, scratch)


def last_turn_kernel(get_table, mine_ref, other_ref, local_ref, *refs, rnd):
    *outs, squares_ref, scratch = refs
    width = local_ref.shape[1] // 2
    first, second = local_ref[:, :width], local_ref[:, width:]
    k, kt = coupling_of(mine_ref[...], other_ref[...], width)
    new = turned([(k, kt, first, -1.0, second), (kt, k, second, 1.0, first)])
    table_ref = get_table()
    me = lax.axis_index("pair")
    squares_ref[...] = jnp.zeros_like(squares_ref)
    for half in range(2):
        scratch[:, half * width : (half + 1) * width] = new[half]
        block = table_ref[rnd, 2 * note(table_ref, NEXT, me) + half]
        sums = jnp.sum(new[half] * new[half], axis=0, keepdims=True)
        for lane in range(0, width, LANES):
            squares_ref[pl.ds((block * width + lane) // LANES, 1), :] = sums[:, lane : lane + LANES]
    rows = outs[0].shape[0]
    for mask, out in enumerate(outs):
        out[...] = scratch[pl.ds(pl.multiple_of((me ^ mask) * rows, rows), rows), :]


def place_kernel(table_ref, *refs, rnd):
    *ins, out_ref = refs
    width = ins[0].shape[1] // 2
    me = lax.axis_index("pair")
    for mask, ref in enumerate(ins):
        for half in range(2):
            block = table_ref[rnd, 2 * note(table_ref, NEXT, me ^ mask) + half]
            start = pl.multiple_of(block * width, width)
            out_ref[:, pl.ds(start, width)] = ref[:, half * width : (half + 1) * width]


def swap(x, axis, mask):
    return lax.ppermute(x, axis, [(i, i ^ mask) for i in range(lax.axis_size(axis))])


def spread(parts):
    return [parts[0]] + [swap(parts[mask], "pair", mask) for mask in range(1, len(parts))]


def tree_sum(parts):
    while len(parts) > 1:
        parts = [a + b for a, b in zip(parts[::2], parts[1::2])]
    return parts[0]


def shares(x, axis, step):
    return [x] + [swap(x, axis, mask) for mask in range(step, lax.axis_size(axis), step)]


def over_chips(x):
    return tree_sum(shares(x, "row", 2))


def powers(size):
    return [1 << bit for bit in range(size.bit_length() - 1)]


def with_late_table(kernel):
    def run(table_vmem, *refs):
        *refs, table_ref, sem = refs
        copy = pltpu.make_async_copy(table_vmem, table_ref, sem)
        copy.start()

        def arrived():
            copy.wait()
            return table_ref

        kernel(arrived, *refs)

    return run


def call(kernel, ins, outs, scratch=(), table=None, late=False, cost=None):
    ins = ([] if table is None else [table]) + ins
    scratch = [pltpu.VMEM(shape, jnp.float32) for shape in scratch]
    if late:
        kernel = with_late_table(kernel)
        scratch += [pltpu.SMEM(table.shape, jnp.int32), pltpu.SemaphoreType.DMA]
    in_smem = table is not None and not late
    return pl.pallas_call(
        kernel,
        out_shape=[jax.ShapeDtypeStruct(shape, jnp.float32) for shape in outs],
        in_specs=[SMEM] * in_smem + [VMEM] * (len(ins) - in_smem),
        out_specs=[VMEM] * len(outs),
        scratch_shapes=scratch,
        compiler_params=pltpu.CompilerParams(vmem_limit_bytes=24 * 2**20),
        cost_estimate=cost,
    )(*ins)


def deal(plan, slab, rnd):
    piece_rows, ncols = slab.shape
    rounds, blocks = plan.shape
    pieces = [jax.ShapeDtypeStruct((piece_rows, 2 * ncols // blocks), jnp.float32)] * (blocks // 2)
    table, *pieces = pl.pallas_call(
        functools.partial(deal_kernel, rnd=rnd),
        out_shape=[jax.ShapeDtypeStruct((rounds + len(NOTES), blocks), jnp.int32)] + pieces,
        in_specs=[HBM, HBM],
        out_specs=[SMEM] + [VMEM] * len(pieces),
        scratch_shapes=[
            pltpu.SMEM(plan.shape, jnp.int32),
            pltpu.VMEM(slab.shape, jnp.float32),
            pltpu.SemaphoreType.DMA,
            pltpu.SemaphoreType.DMA,
        ],
        compiler_params=pltpu.CompilerParams(vmem_limit_bytes=58 * 2**20),
    )(plan, slab)
    return table, pieces


def on_device(slab, plan):
    piece_rows, ncols = slab.shape
    pair_count = lax.axis_size("pair")
    both = ncols // pair_count
    width = both // 2
    group_rows = piece_rows * pair_count
    total_rows = group_rows * lax.axis_size("row")
    crossed = [(group_rows, both), parts_of(width), parts_of(width)]
    square = (width, width)
    masks = powers(pair_count) if pair_count <= 4 else list(range(1, pair_count))
    rest = [mask for mask in range(1, pair_count) if mask not in masks]

    table, dealt = deal(plan, slab, 0)
    own, *others = spread(dealt)
    own = call(copy_kernel, [own], [own.shape])
    local, keep, send = call(first_cross_kernel, [*own, *others], crossed, [square])
    own, *ahead = call(
        functools.partial(ahead_kernel, rnd=0, masks=masks, rest=rest),
        [slab, local],
        [(piece_rows, both)] + [((1 + len(rest)) * piece_rows, both)] * len(masks),
        table=table,
    )
    total, ahead = lax.optimization_barrier((keep + swap(send, "row", 1), ahead))
    raw = [swap(x, "pair", mask) for x, mask in zip(ahead, masks)]
    mine, raw = lax.optimization_barrier((over_chips(total), raw))
    came = [swap(mine, "pair", mask) for mask in masks]
    came_other = [swap(x, "row", 1) for x in came]
    local, keep, send = call(
        functools.partial(turn_kernel, rnd=0, masks=masks, rest=rest),
        [mine, swap(mine, "row", 1), local, own] + came + came_other + raw,
        crossed,
        [square, (group_rows, both)],
        table,
        late=True,
    )
    mine = over_chips(keep + swap(send, "row", 1))
    *sent, squares = call(
        functools.partial(last_turn_kernel, rnd=1),
        [mine, swap(mine, "row", 1), local],
        [(piece_rows, both)] * pair_count + [(ncols // LANES, LANES)],
        [(group_rows, both)],
        table,
        late=True,
    )
    squares, first_sent = lax.optimization_barrier((squares, sent[1]))
    back = [sent[0], swap(first_sent, "pair", 1)]
    squares = squares + swap(squares, "row", 1)
    squares, sent = lax.optimization_barrier((squares, sent))
    back += [swap(sent[mask], "pair", mask) for mask in range(2, pair_count)]
    parts, back[1] = lax.optimization_barrier((shares(squares, "row", 2), back[1]))
    squares = tree_sum(shares(tree_sum(parts), "pair", 1))
    (rotated,) = call(
        functools.partial(place_kernel, rnd=1),
        back,
        [(piece_rows, ncols)],
        table=table,
        cost=pl.CostEstimate(flops=0, bytes_accessed=8 * slab.size, transcendentals=0),
    )
    return rotated, jnp.sqrt(squares / total_rows).reshape(ncols)


def solution(mesh):
    specs = (P(("row", "pair"), None), P())
    return jax.shard_map(on_device, mesh=mesh, in_specs=specs, out_specs=specs, check_vma=False)
```
